128 devices in a mesh: row: 16 (over x, y_hi, core), col: 8 (over y_lo, z).
Axes of the slice: x: 4, y: 4 (y_hi: 2, y_lo: 2; y = y_hi * 2 + y_lo), z: 4, core: 2. Of those that a mesh axis runs over, the one named last changes fastest.
Arguments:
- vectors_in: float32 [1024, 196608], P(('row', 'col')), may hold values from -6 to 6
- panel_first: float32 [196608, 256], P('row', 'col'), may hold values from -0.15625 to 0.15625
- panel_second: float32 [196608, 256], P('row', 'col'), may hold values from -0.15625 to 0.15625
- factor_first: float32 [256, 256], replicated, may hold values from -0.375 to 0.375
- factor_second: float32 [256, 256], replicated, may hold values from -0.375 to 0.375
Outputs:
- vectors_out: float32 [1024, 196608], P('col', 'row')
The draws below stay inside these ranges and needn't reach their ends.
All inputs are finite; a program needn't handle non-finite values.
Results may differ from the reference program's by a relative error of at most 0.00007.
Values sent between devices are 32-bit elements; how exact they have to be, the bound alone decides.
No kernel may reach another device: no remote copies, remote signals or barrier semaphores. Data moves between devices by JAX's collectives and lax.ppermute only.
A program may use at most 192 MiB of HBM per device.

```python
import jax
import jax.numpy as jnp
from jax import lax

N = 196608
K = 1024
PW = 256


def steps_of(stream_key, extent, cuts, smallest, top_value):
    loudness = 1.0
    for axis_at, parts in cuts:
        heights = jax.random.uniform(jax.random.fold_in(jax.random.fold_in(stream_key, 6), axis_at), (parts,), jnp.float32, smallest / len(cuts), top_value / len(cuts))
        loudness = loudness * jnp.repeat(jnp.exp(heights), extent[axis_at] // parts).reshape((-1,) + (1,) * (len(extent) - 1 - axis_at))
    return loudness


def gaussian(own_key, shape, scale, bound, split=(), kind=jnp.bfloat16):
    loudness = steps_of(own_key, shape, split, -0.22, 0.18) if split else 1.0
    values = jax.random.normal(own_key, shape, jnp.float32) * scale * loudness
    return jnp.minimum(jnp.maximum(values, -bound), bound).astype(kind)


def setup_inputs(seed: int = 0) -> dict:
    key_of = jax.random.split(jax.random.key(seed), 6)
    vectors_in = gaussian(key_of[0], (K, N), 1.0, 6.0, ((0, 128),), jnp.float32)
    panel_first = gaussian(key_of[1], (N, PW), ((512 * N) ** -0.25), 0.15625, ((0, 16), (1, 8)), jnp.float32)
    panel_second = gaussian(key_of[2], (N, PW), ((512 * N) ** -0.25), 0.15625, ((0, 16), (1, 8)), jnp.float32)
    factor_first = gaussian(key_of[3], (PW, PW), PW ** -0.5, 0.375, (), jnp.float32)
    factor_second = gaussian(key_of[4], (PW, PW), PW ** -0.5, 0.375, (), jnp.float32)
    return dict(vectors_in=vectors_in, panel_first=panel_first, panel_second=panel_second, factor_first=factor_first, factor_second=factor_second)


def apply_one(zt, panel, factor):
    hp = lax.Precision.HIGHEST
    w = jnp.dot(zt, panel, precision=hp, preferred_element_type=jnp.float32)
    tw = jnp.dot(w, factor.T, precision=hp, preferred_element_type=jnp.float32)
    update = lax.dot_general(tw, panel, (((1,), (1,)), ((), ())), precision=hp, preferred_element_type=jnp.float32)
    return zt - update


def reference(vectors_in, panel_first, panel_second, factor_first, factor_second):
    zt = apply_one(vectors_in, panel_first, factor_first)
    return apply_one(zt, panel_second, factor_second)
```

```python
import jax
import jax.numpy as jnp
from jax import lax
from jax.sharding import Mesh, PartitionSpec as P

CHIPS = ("block", "col")
CORES = 2


def dot(left, right, left_dim, right_dim, precision):
    return lax.dot_general(
        left,
        right,
        (((left_dim,), (right_dim,)), ((), ())),
        precision=precision,
        preferred_element_type=jnp.float32,
    )


def body(vectors_in, panel_first, panel_second, factor_first, factor_second):
    blocks, cols = lax.axis_size("block"), lax.axis_size("col")
    chips = blocks * cols
    held = vectors_in.shape[0]
    width = panel_first.shape[1] * cols
    part = panel_first.shape[0] // cols
    core = lax.axis_index("core")

    panels = jnp.concatenate([panel_first.T, panel_second.T], axis=0)
    panels = panels.reshape(-1, cols, part).transpose(1, 0, 2)
    own = lax.all_to_all(panels, "col", split_axis=0, concat_axis=0, tiled=True)
    other = lax.ppermute(own, "core", [(0, 1), (1, 0)])
    zero = core == 0
    panels = jnp.stack([jnp.where(zero, own, other), jnp.where(zero, other, own)], axis=2)
    panels = panels.reshape(cols, 2, width // cols, CORES * part)
    panels = panels.transpose(1, 0, 2, 3).reshape(2 * width, CORES * part)
    overlap = dot(panels[:width], panels[width:], 1, 1, lax.Precision.HIGHEST)

    zt = vectors_in.reshape(held, blocks, CORES, cols, part).transpose(1, 3, 0, 2, 4)
    zt = zt.reshape(chips, held, CORES * part)
    zt = lax.all_to_all(zt, CHIPS, split_axis=0, concat_axis=0, tiled=True)
    zt = zt.reshape(chips * held, CORES * part)

    partial = dot(zt, panels, 1, 1, lax.Precision.HIGH).reshape(chips, held, 2 * width)
    partial = jnp.concatenate([partial, overlap.reshape(chips, held, -1)], axis=2)
    pieces = lax.all_to_all(partial, CHIPS, split_axis=0, concat_axis=0, tiled=True)
    total = jnp.sum(pieces, axis=0)
    copies = jnp.broadcast_to(total[None], (chips,) + total.shape)
    total = lax.all_to_all(copies, CHIPS, split_axis=0, concat_axis=0, tiled=True)
    overlap = total[:, :, 2 * width :].reshape(width, width)
    total = total.reshape(chips * held, -1)
    first = dot(total[:, :width], factor_first, 1, 1, lax.Precision.HIGHEST)
    second = total[:, width : 2 * width] - dot(first, overlap, 1, 0, lax.Precision.HIGHEST)
    second = dot(second, factor_second, 1, 1, lax.Precision.HIGHEST)
    weights = jnp.concatenate([first, second], axis=1)

    zt = zt - dot(weights, panels, 1, 0, lax.Precision.HIGH)
    zt = zt.reshape(blocks, cols * held, CORES, part).transpose(2, 0, 1, 3)
    zt = zt.reshape(CORES * cols, cols * held, part)
    zt = lax.all_to_all(zt, ("core", "col"), split_axis=0, concat_axis=0, tiled=True)
    zt = zt.reshape(CORES, cols, cols * held, part).transpose(0, 2, 1, 3)
    return zt.reshape(CORES * cols * held, cols * part)


def solution(mesh):
    rows, cols = mesh.devices.shape
    split = Mesh(mesh.devices.reshape(rows // CORES, CORES, cols), ("block", "core", "col"))
    return jax.shard_map(
        body,
        mesh=split,
        in_specs=(
            P(("block", "core", "col"), None),
            P(("block", "core"), "col"),
            P(("block", "core"), "col"),
            P(),
            P(),
        ),
        out_specs=P("col", ("block", "core")),
        check_vma=False,
    )
```

```python
import jax
import jax.numpy as jnp
from jax import lax
from jax.experimental import pallas as pl
from jax.experimental.pallas import tpu as pltpu
from jax.sharding import Mesh, PartitionSpec as P

CHIPS = ("block", "half", "place")
INNER = ("core", "half", "place")
CORES = 2
HALVES = 2
VMEM_LIMIT = 48 * 1024 * 1024
ANY = pl.BlockSpec(memory_space=pl.ANY)
SCALAR = pl.BlockSpec(memory_space=pltpu.SMEM)


def f32(*shape):
    return jax.ShapeDtypeStruct(shape, jnp.float32)


def params():
    return pltpu.CompilerParams(vmem_limit_bytes=VMEM_LIMIT)


def in_two(values):
    high = values.astype(jnp.bfloat16)
    return high, (values - high.astype(jnp.float32)).astype(jnp.bfloat16)


def dot3(left, right, right_dim):
    (lh, ll), (rh, rl) = left, right

    def dot(a, b):
        return lax.dot_general(
            a, b, (((1,), (right_dim,)), ((), ())), preferred_element_type=jnp.float32
        )

    return dot(lh, rh) + (dot(lh, rl) + dot(ll, rh))


def dot(left, right, left_dim, right_dim):
    return lax.dot_general(
        left,
        right,
        (((left_dim,), (right_dim,)), ((), ())),
        precision=lax.Precision.HIGHEST,
        preferred_element_type=jnp.float32,
    )


def copy_all(copies):
    for one in copies:
        one.start()
    for one in copies:
        one.wait()


def partner(place, j, core, half):
    return place ^ j ^ (2 * (core ^ half))


def times(index, size):
    return pl.ds(pl.multiple_of(index * size, size), size)


def pack_panels(where, first, second, order):
    held, rows = first.shape
    places = len(order)
    part = rows // places

    def kernel(where_ref, first_ref, second_ref, *rest):
        outs, sems = rest[:places], rest[places]
        copies = []
        for i, j in enumerate(order):
            at = times(partner(where_ref[2], j, where_ref[0], where_ref[1]), part)
            for p, ref in enumerate((first_ref, second_ref)):
                target = outs[i].at[pl.ds(p * held, held)]
                copies.append(pltpu.make_async_copy(ref.at[:, at], target, sems.at[2 * i + p]))
        copy_all(copies)

    return pl.pallas_call(
        kernel,
        out_shape=[f32(2 * held, part)] * places,
        in_specs=[SCALAR, ANY, ANY],
        out_specs=[ANY] * places,
        scratch_shapes=[pltpu.SemaphoreType.DMA((2 * places,))],
        compiler_params=params(),
        name="pack_panels",
    )(where, first, second)


def join_panels(where, pieces, order):
    places = len(order)
    held, part = pieces[0].shape[0] // 2, pieces[0].shape[1]

    def kernel(where_ref, *rest):
        ins, out, sems = rest[:places], rest[places], rest[places + 1]
        copies = []
        for i, j in enumerate(order):
            at = times(partner(where_ref[2], j, where_ref[0], where_ref[1]), held)
            for p in range(2):
                source = ins[i].at[pl.ds(p * held, held)]
                copies.append(pltpu.make_async_copy(source, out.at[p, at], sems.at[2 * i + p]))
        copy_all(copies)

    return pl.pallas_call(
        kernel,
        out_shape=f32(2, places * held, part),
        in_specs=[SCALAR] + [ANY] * places,
        out_specs=ANY,
        scratch_shapes=[pltpu.SemaphoreType.DMA((2 * places,))],
        compiler_params=params(),
        name="join_panels",
    )(where, *pieces)


def prepare(where, own, other, chips, held):
    _, count, rows = own.shape
    width = CORES * count
    steps = 6
    tile = rows // steps

    def kernel(where_ref, own_ref, other_ref, high_ref, low_ref, out_ref, overlap_ref):
        step = pl.program_id(0)

        @pl.when(step == 0)
        def _():
            overlap_ref[...] = jnp.zeros_like(overlap_ref)

        for p in range(2):
            for d, ref in enumerate((own_ref, other_ref)):
                at = times(p * CORES + (where_ref[0] ^ d), count)
                high_ref[at], low_ref[at] = in_two(ref[p])
        first, second = ((high_ref[at], low_ref[at]) for at in (pl.ds(0, width), pl.ds(width, width)))
        overlap_ref[...] += dot3(first, second, 1)

        @pl.when(step == steps - 1)
        def _():
            half = chips // 2
            out_ref[:half] = overlap_ref[:, :count].reshape(half, held, count)
            out_ref[half:] = overlap_ref[:, count:].reshape(half, held, count)

    panels = pl.BlockSpec((2, count, tile), lambda i, w: (0, 0, i))
    part = pl.BlockSpec((2 * width, tile), lambda i, w: (0, i))
    bf16 = jax.ShapeDtypeStruct((2 * width, rows), jnp.bfloat16)
    return pl.pallas_call(
        kernel,
        out_shape=[bf16, bf16, f32(chips, held, count)],
        grid_spec=pltpu.PrefetchScalarGridSpec(
            num_scalar_prefetch=1,
            grid=(steps,),
            in_specs=[panels, panels],
            out_specs=[part, part, pl.BlockSpec((chips, held, count), lambda i, w: (0, 0, 0))],
            scratch_shapes=[pltpu.VMEM((width, width), jnp.float32)],
        ),
        compiler_params=params(),
        name="prepare",
    )(where, own, other)


def project(zt, high, low, overlap):
    vectors, rows = zt.shape
    both = high.shape[0]
    chips, held, more = overlap.shape
    steps = 6
    tile = rows // steps

    def kernel(z_ref, high_ref, low_ref, overlap_ref, out_ref, sum_ref):
        step = pl.program_id(0)

        @pl.when(step == 0)
        def _():
            sum_ref[...] = jnp.zeros_like(sum_ref)

        sum_ref[...] += dot3(in_two(z_ref[...]), (high_ref[...], low_ref[...]), 1)

        @pl.when(step == steps - 1)
        def _():
            out_ref[:, :, :both] = sum_ref[...].reshape(chips, held, both)
            out_ref[:, :, both:] = overlap_ref[...]

    tiles = pl.BlockSpec((both, tile), lambda i: (0, i))
    return pl.pallas_call(
        kernel,
        out_shape=f32(chips, held, both + more),
        grid=(steps,),
        in_specs=[
            pl.BlockSpec((vectors, tile), lambda i: (0, i)),
            tiles,
            tiles,
            pl.BlockSpec((chips, held, more), lambda i: (0, 0, 0)),
        ],
        out_specs=pl.BlockSpec((chips, held, both + more), lambda i: (0, 0, 0)),
        scratch_shapes=[pltpu.VMEM((vectors, both), jnp.float32)],
        compiler_params=params(),
        name="project",
    )(zt, high, low, overlap)


def update(where, zt, weights, high, low, flip, order):
    vectors, rows = zt.shape
    both = high.shape[0]
    places = len(order)
    block = vectors // (HALVES * places)
    steps = 6
    tile = rows // steps

    def target(w, j):
        return (w[0] ^ flip) * places + partner(w[2], j, w[0], w[1])

    def kernel(where_ref, *refs):
        z_refs, (weights_ref, high_ref, low_ref), outs = refs[:places], refs[places:-places], refs[-places:]
        rows = [weights_ref[times(target(where_ref, j), block)] for j in order]
        change = dot3(in_two(jnp.concatenate(rows, axis=0)), (high_ref[...], low_ref[...]), 0)
        for i in range(places):
            outs[i][...] = z_refs[i][...] - change[i * block : (i + 1) * block]

    def z_spec(j):
        return pl.BlockSpec((block, tile), lambda i, w: (target(w, j), i))

    tiles = pl.BlockSpec((both, tile), lambda i, w: (0, i))
    return pl.pallas_call(
        kernel,
        out_shape=[f32(block, rows)] * places,
        grid_spec=pltpu.PrefetchScalarGridSpec(
            num_scalar_prefetch=1,
            grid=(steps,),
            in_specs=[z_spec(j) for j in order]
            + [pl.BlockSpec((vectors, both), lambda i, w: (0, 0)), tiles, tiles],
            out_specs=[pl.BlockSpec((block, tile), lambda i, w: (0, i))] * places,
        ),
        compiler_params=params(),
        name="update",
    )(where, *[zt] * places, weights, high, low)


def gather(where, pieces, names, places, out=None):
    block, part = pieces[0].shape
    n = len(pieces)

    def kernel(where_ref, *refs):
        ins, dst, sems = refs[:n], refs[-2], refs[-1]
        copies = []
        for i, (flip, j) in enumerate(names):
            core = where_ref[1] ^ flip
            target = dst.at[times(core, block), times(partner(where_ref[2], j, where_ref[0], core), part)]
            copies.append(pltpu.make_async_copy(ins[i], target, sems.at[i]))
        copy_all(copies)

    held = [] if out is None else [out]
    return pl.pallas_call(
        kernel,
        out_shape=f32(CORES * block, places * part),
        in_specs=[SCALAR] + [ANY] * (n + len(held)),
        out_specs=ANY,
        scratch_shapes=[pltpu.SemaphoreType.DMA((n,))],
        input_output_aliases={n + 1: 0} if held else {},
        compiler_params=params(),
        name="gather",
    )(where, *pieces, *held)


def body(vectors_in, panel_first, panel_second, factor_first, factor_second):
    blocks, places = lax.axis_size("block"), lax.axis_size("place")
    chips = blocks * HALVES * places
    held = vectors_in.shape[0]
    width = panel_first.shape[1] * HALVES * places
    where = jnp.stack([lax.axis_index(name) for name in INNER]).astype(jnp.int32)

    def permute(piece, target):
        index = [(c, h, p) for c in range(CORES) for h in range(HALVES) for p in range(places)]
        return lax.ppermute(piece, INNER, [(i, index.index(target(*at))) for i, at in enumerate(index)])

    order = (3, 1, 0, 2)
    pieces = pack_panels(where, panel_first.T, panel_second.T, order)
    pieces = [
        permute(piece, lambda c, h, p: (h, c, partner(p, j, c, h))) for j, piece in zip(order, pieces)
    ]
    vectors_in, pieces = lax.optimization_barrier((vectors_in, pieces))
    zt = lax.all_to_all(vectors_in, CHIPS, split_axis=1, concat_axis=0, tiled=True)
    own = join_panels(where, pieces, order)
    other = lax.ppermute(own, "core", [(0, 1), (1, 0)])
    high, low, overlap = prepare(where, own, other, chips, held)

    partial = project(zt, high, low, overlap)
    parts = lax.all_to_all(partial, CHIPS, split_axis=0, concat_axis=0, tiled=True)
    total = jnp.sum(parts, axis=0)
    copies = jnp.broadcast_to(total[None], (chips,) + total.shape)
    total = lax.all_to_all(copies, CHIPS, split_axis=0, concat_axis=0, tiled=True)
    overlap = total[:, :, 2 * width :].reshape(2, width, -1)
    overlap = jnp.concatenate([overlap[0], overlap[1]], axis=1)
    total = total.reshape(chips * held, -1)
    first = dot(total[:, :width], factor_first, 1, 1)
    second = total[:, width : 2 * width] - dot(first, overlap, 1, 0)
    second = dot(second, factor_second, 1, 1)
    weights = jnp.concatenate([first, second], axis=1)

    out = None
    for flip in range(HALVES):
        pieces = update(where, zt, weights, high, low, flip, order)
        pieces = [
            permute(piece, lambda c, h, p: (h, c ^ flip, partner(p, j, c, h)))
            for j, piece in zip(order, pieces)
        ]
        out = gather(where, pieces, [(flip, j) for j in order], places, out)
    return out


def solution(mesh):
    rows, cols = mesh.devices.shape
    blocks, places = rows // CORES, cols // HALVES
    split = Mesh(mesh.devices.reshape(blocks, CORES, HALVES, places), ("block",) + INNER)
    row, col = ("block", "core"), ("half", "place")
    return jax.shard_map(
        body,
        mesh=split,
        in_specs=(P(row + col, None), P(row, col), P(row, col), P(), P()),
        out_specs=P(col, row),
        check_vma=False,
    )
```

```python
import jax
import jax.numpy as jnp
from jax import lax
from jax.experimental import pallas as pl
from jax.experimental.pallas import tpu as pltpu
from jax.sharding import Mesh, PartitionSpec as P

CHIPS = ("block", "half", "place")
INNER = ("core", "half", "place")
CORES = 2
HALVES = 2
VMEM_LIMIT = 24 * 1024 * 1024
ANY = pl.BlockSpec(memory_space=pl.ANY)
WHOLE = pl.BlockSpec(memory_space=pltpu.VMEM)
SCALAR = pl.BlockSpec(memory_space=pltpu.SMEM)


def f32(*shape):
    return jax.ShapeDtypeStruct(shape, jnp.float32)


def params():
    return pltpu.CompilerParams(vmem_limit_bytes=VMEM_LIMIT)


def in_two(values):
    high = values.astype(jnp.bfloat16)
    return high, (values - high.astype(jnp.float32)).astype(jnp.bfloat16)


def dot3(left, right, right_dim):
    (lh, ll), (rh, rl) = left, right

    def dot(a, b):
        return lax.dot_general(
            a, b, (((1,), (right_dim,)), ((), ())), preferred_element_type=jnp.float32
        )

    return dot(lh, rh) + (dot(lh, rl) + dot(ll, rh))


def copy_all(copies):
    for one in copies:
        one.start()
    for one in copies:
        one.wait()


def partner(place, j, core, half):
    return place ^ j ^ (2 * (core ^ half))


def times(index, size):
    return pl.ds(pl.multiple_of(index * size, size), size)


def pack_panels(where, first, second, order, places):
    held, rows = first.shape
    part = rows // places
    count = len(order)

    def kernel(where_ref, *refs):
        for i, out in enumerate(refs[2 * count :]):
            out[:held] = refs[2 * i][...]
            out[held:] = refs[2 * i + 1][...]

    def spec(j):
        return pl.BlockSpec((held, part), lambda i, w: (0, partner(w[2], j, w[0], w[1])))

    return pl.pallas_call(
        kernel,
        out_shape=[f32(2 * held, part)] * count,
        grid_spec=pltpu.PrefetchScalarGridSpec(
            num_scalar_prefetch=1,
            grid=(1,),
            in_specs=[spec(j) for j in order for _ in range(2)],
            out_specs=[pl.BlockSpec((2 * held, part), lambda i, w: (0, 0))] * count,
        ),
        compiler_params=params(),
        name="pack_panels",
    )(where, *[first, second] * count)


def prepare(where, own, other, order, chips, held):
    places = len(order)
    held_cols, rows = own[0].shape[0] // 2, own[0].shape[1]
    count = places * held_cols
    width = CORES * count
    steps = 6
    tile = rows // steps

    def kernel(where_ref, *refs):
        ins, (high_ref, low_ref, out_ref, overlap_ref) = refs[: 2 * places], refs[2 * places :]
        step = pl.program_id(0)

        @pl.when(step == 0)
        def _():
            overlap_ref[...] = jnp.zeros_like(overlap_ref)

        for d in range(CORES):
            core = where_ref[0] ^ d
            for i, j in enumerate(order):
                place = partner(where_ref[2], j, core, where_ref[1])
                for p in range(2):
                    at = times((p * CORES + core) * places + place, held_cols)
                    values = ins[d * places + i][pl.ds(p * held_cols, held_cols)]
                    high_ref[at], low_ref[at] = in_two(values)
        first, second = ((high_ref[at], low_ref[at]) for at in (pl.ds(0, width), pl.ds(width, width)))
        overlap_ref[...] += dot3(first, second, 1)

        @pl.when(step == steps - 1)
        def _():
            half = chips // 2
            out_ref[:half] = overlap_ref[:, :count].reshape(half, held, count)
            out_ref[half:] = overlap_ref[:, count:].reshape(half, held, count)

    piece = pl.BlockSpec((2 * held_cols, tile), lambda i, w: (0, i))
    part = pl.BlockSpec((2 * width, tile), lambda i, w: (0, i))
    bf16 = jax.ShapeDtypeStruct((2 * width, rows), jnp.bfloat16)
    return pl.pallas_call(
        kernel,
        out_shape=[bf16, bf16, f32(chips, held, count)],
        grid_spec=pltpu.PrefetchScalarGridSpec(
            num_scalar_prefetch=1,
            grid=(steps,),
            in_specs=[piece] * (2 * places),
            out_specs=[part, part, pl.BlockSpec((chips, held, count), lambda i, w: (0, 0, 0))],
            scratch_shapes=[pltpu.VMEM((width, width), jnp.float32)],
        ),
        compiler_params=params(),
        name="prepare",
    )(where, *own, *other)


def project(zt, high, low, overlap):
    vectors, rows = zt.shape
    both = high.shape[0]
    chips, held, more = overlap.shape
    steps = 2

    def kernel(z_ref, high_ref, low_ref, overlap_ref, out_ref):
        sums = dot3(in_two(z_ref[...]), (high_ref[...], low_ref[...]), 1)
        out_ref[:, :, :both] = sums.reshape(chips // steps, held, both)
        out_ref[:, :, both:] = overlap_ref[...]

    return pl.pallas_call(
        kernel,
        out_shape=f32(chips, held, both + more),
        grid=(steps,),
        in_specs=[
            pl.BlockSpec((vectors // steps, rows), lambda i: (i, 0)),
            WHOLE,
            WHOLE,
            pl.BlockSpec((chips // steps, held, more), lambda i: (i, 0, 0)),
        ],
        out_specs=pl.BlockSpec((chips // steps, held, both + more), lambda i: (i, 0, 0)),
        compiler_params=params(),
        name="project",
    )(zt, high, low, overlap)


def add_up(parts):
    def kernel(in_ref, out_ref):
        out_ref[...] = jnp.broadcast_to(jnp.sum(in_ref[...], axis=0, keepdims=True), out_ref.shape)

    return pl.pallas_call(
        kernel,
        out_shape=f32(*parts.shape),
        in_specs=[WHOLE],
        out_specs=WHOLE,
        compiler_params=params(),
        name="add_up",
    )(parts)


def solve(total, factor_first, factor_second):
    chips, held, more = total.shape
    width = factor_first.shape[0]
    cut = width // 2
    full = lax.Precision.HIGHEST
    rows = (((1,), (1,)), ((), ()))

    def kernel(total_ref, first_ref, second_ref, out_ref):
        pieces = total_ref[:, :, 2 * width :].reshape(2, width, cut)
        overlap = jnp.concatenate([pieces[0], pieces[1]], axis=1)
        first = total_ref[:, :, :width].reshape(chips * held, width)
        second = total_ref[:, :, width : 2 * width].reshape(chips * held, width)
        first = lax.dot_general(first, first_ref[...], rows, precision=full)
        second = second - jnp.dot(first, overlap, precision=full)
        out_ref[:, :width] = first
        out_ref[:, width:] = lax.dot_general(second, second_ref[...], rows, precision=full)

    return pl.pallas_call(
        kernel,
        out_shape=f32(chips * held, 2 * width),
        in_specs=[WHOLE] * 3,
        out_specs=WHOLE,
        compiler_params=params(),
        name="solve",
    )(total, factor_first, factor_second)


def update(where, zt, weights, high, low, flip, order, places):
    vectors, rows = zt.shape
    block = vectors // (HALVES * places)
    count = len(order)

    def target(w, j):
        return (w[0] ^ flip) * places + partner(w[2], j, w[0], w[1])

    def kernel(where_ref, *refs):
        z_refs, (weights_ref, high_ref, low_ref), outs = refs[:count], refs[count:-count], refs[-count:]
        rows = [weights_ref[times(target(where_ref, j), block)] for j in order]
        change = dot3(in_two(jnp.concatenate(rows, axis=0)), (high_ref[...], low_ref[...]), 0)
        for i in range(count):
            outs[i][...] = z_refs[i][...] - change[i * block : (i + 1) * block]

    def z_spec(j):
        return pl.BlockSpec((block, rows), lambda i, w: (target(w, j), 0))

    return pl.pallas_call(
        kernel,
        out_shape=[f32(block, rows)] * count,
        grid_spec=pltpu.PrefetchScalarGridSpec(
            num_scalar_prefetch=1,
            grid=(1,),
            in_specs=[z_spec(j) for j in order] + [WHOLE] * 3,
            out_specs=[pl.BlockSpec((block, rows), lambda i, w: (0, 0))] * count,
        ),
        compiler_params=params(),
        name="update",
    )(where, *[zt] * count, weights, high, low)


def gather(where, pieces, names, places, out=None):
    block, part = pieces[0].shape
    n = len(pieces)

    def kernel(where_ref, *refs):
        ins, dst, sems = refs[:n], refs[-2], refs[-1]
        copies = []
        for i, (flip, j) in enumerate(names):
            core = where_ref[1] ^ flip
            target = dst.at[times(core, block), times(partner(where_ref[2], j, where_ref[0], core), part)]
            copies.append(pltpu.make_async_copy(ins[i], target, sems.at[i]))
        copy_all(copies)

    held = [] if out is None else [out]
    return pl.pallas_call(
        kernel,
        out_shape=f32(CORES * block, places * part),
        in_specs=[SCALAR] + [ANY] * (n + len(held)),
        out_specs=ANY,
        scratch_shapes=[pltpu.SemaphoreType.DMA((n,))],
        input_output_aliases={n + 1: 0} if held else {},
        compiler_params=params(),
        name="gather",
    )(where, *pieces, *held)


def body(vectors_in, panel_first, panel_second, factor_first, factor_second):
    blocks, places = lax.axis_size("block"), lax.axis_size("place")
    chips = blocks * HALVES * places
    held = vectors_in.shape[0]
    where = jnp.stack([lax.axis_index(name) for name in INNER]).astype(jnp.int32)

    def permute(piece, target):
        index = [(c, h, p) for c in range(CORES) for h in range(HALVES) for p in range(places)]
        return lax.ppermute(piece, INNER, [(i, index.index(target(*at))) for i, at in enumerate(index)])

    order = (3, 1, 0, 2)
    pieces = pack_panels(where, panel_first.T, panel_second.T, order[:2], places)
    pieces += pack_panels(where, panel_first.T, panel_second.T, order[2:], places)
    own = [permute(piece, lambda c, h, p: (h, c, partner(p, j, c, h))) for j, piece in zip(order, pieces)]
    other = [lax.ppermute(piece, "core", [(0, 1), (1, 0)]) for piece in own]
    vectors_in, own, other = lax.optimization_barrier((vectors_in, own, other))
    zt = lax.all_to_all(vectors_in, CHIPS, split_axis=1, concat_axis=0, tiled=True)
    zt = zt.reshape(chips * held, -1)
    zt, own, other = lax.optimization_barrier((zt, own, other))
    high, low, overlap = prepare(where, own, other, order, chips, held)

    partial = project(zt, high, low, overlap)
    parts = lax.all_to_all(partial, CHIPS, split_axis=0, concat_axis=0, tiled=True)
    total = lax.all_to_all(add_up(parts), CHIPS, split_axis=0, concat_axis=0, tiled=True)
    weights = solve(total, factor_first, factor_second)

    pieces, names = [], []
    for flip in range(HALVES):
        for some in (order[:2], order[2:]):
            for j, piece in zip(some, update(where, zt, weights, high, low, flip, some, places)):
                pieces.append(permute(piece, lambda c, h, p: (h, c ^ flip, partner(p, j, c, h))))
                names.append((flip, j))
    out = None
    for some in (slice(0, 4), slice(4, 7), slice(7, 8)):
        out = gather(where, pieces[some], names[some], places, out)
    return out


def solution(mesh):
    rows, cols = mesh.devices.shape
    blocks, places = rows // CORES, cols // HALVES
    split = Mesh(mesh.devices.reshape(blocks, CORES, HALVES, places), ("block",) + INNER)
    row, col = ("block", "core"), ("half", "place")
    return jax.shard_map(
        body,
        mesh=split,
        in_specs=(P(row + col, None), P(row, col), P(row, col), P(), P()),
        out_specs=P(col, row),
        check_vma=False,
    )
```

```python
import jax
import jax.numpy as jnp
from jax import lax
from jax.experimental import pallas as pl
from jax.experimental.pallas import tpu as pltpu
from jax.sharding import Mesh, PartitionSpec as P

CHIPS = ("block", "half", "place")
INNER = ("core", "half", "place")
CORES = 2
HALVES = 2
VMEM_LIMIT = 24 * 1024 * 1024
ANY = pl.BlockSpec(memory_space=pl.ANY)
WHOLE = pl.BlockSpec(memory_space=pltpu.VMEM)
SCALAR = pl.BlockSpec(memory_space=pltpu.SMEM)


def f32(*shape):
    return jax.ShapeDtypeStruct(shape, jnp.float32)


def params():
    return pltpu.CompilerParams(vmem_limit_bytes=VMEM_LIMIT)


def in_two(values):
    high = values.astype(jnp.bfloat16)
    return high, (values - high.astype(jnp.float32)).astype(jnp.bfloat16)


def dot3(left, right, right_dim):
    (lh, ll), (rh, rl) = left, right

    def dot(a, b):
        return lax.dot_general(
            a, b, (((1,), (right_dim,)), ((), ())), preferred_element_type=jnp.float32
        )

    return dot(lh, rh) + (dot(lh, rl) + dot(ll, rh))


def copy_all(copies):
    for one in copies:
        one.start()
    for one in copies:
        one.wait()


def partner(place, j, core, half):
    return place ^ j ^ (2 * (core ^ half))


def times(index, size):
    return pl.ds(pl.multiple_of(index * size, size), size)


def pack_panels(where, first, second, order, places):
    held, rows = first.shape
    part = rows // places
    count = len(order)

    def kernel(where_ref, *refs):
        for i, out in enumerate(refs[2 * count :]):
            out[:held] = refs[2 * i][...]
            out[held:] = refs[2 * i + 1][...]

    def spec(j):
        return pl.BlockSpec((held, part), lambda i, w: (0, partner(w[2], j, w[0], w[1])))

    return pl.pallas_call(
        kernel,
        out_shape=[f32(2 * held, part)] * count,
        grid_spec=pltpu.PrefetchScalarGridSpec(
            num_scalar_prefetch=1,
            grid=(1,),
            in_specs=[spec(j) for j in order for _ in range(2)],
            out_specs=[pl.BlockSpec((2 * held, part), lambda i, w: (0, 0))] * count,
        ),
        compiler_params=params(),
        name="pack_panels",
    )(where, *[first, second] * count)


def prepare(where, own, other, order, chips, held):
    places = len(order)
    held_cols, rows = own[0].shape[0] // 2, own[0].shape[1]
    count = places * held_cols
    width = CORES * count
    steps = 2
    tile = rows // steps

    def kernel(where_ref, *refs):
        ins, (high_ref, low_ref, out_ref, overlap_ref) = refs[: 2 * places], refs[2 * places :]
        step = pl.program_id(0)

        @pl.when(step == 0)
        def _():
            overlap_ref[...] = jnp.zeros_like(overlap_ref)

        for d in range(CORES):
            core = where_ref[0] ^ d
            for i, j in enumerate(order):
                place = partner(where_ref[2], j, core, where_ref[1])
                for p in range(2):
                    at = times((p * CORES + core) * places + place, held_cols)
                    values = ins[d * places + i][pl.ds(p * held_cols, held_cols)]
                    high_ref[at], low_ref[at] = in_two(values)
        first, second = ((high_ref[at], low_ref[at]) for at in (pl.ds(0, width), pl.ds(width, width)))
        overlap_ref[...] += dot3(first, second, 1)

        @pl.when(step == steps - 1)
        def _():
            half = chips // 2
            out_ref[:half] = overlap_ref[:, :count].reshape(half, held, count)
            out_ref[half:] = overlap_ref[:, count:].reshape(half, held, count)

    piece = pl.BlockSpec((2 * held_cols, tile), lambda i, w: (0, i))
    part = pl.BlockSpec((2 * width, tile), lambda i, w: (0, i))
    bf16 = jax.ShapeDtypeStruct((2 * width, rows), jnp.bfloat16)
    return pl.pallas_call(
        kernel,
        out_shape=[bf16, bf16, f32(chips, held, count)],
        grid_spec=pltpu.PrefetchScalarGridSpec(
            num_scalar_prefetch=1,
            grid=(steps,),
            in_specs=[piece] * (2 * places),
            out_specs=[part, part, pl.BlockSpec((chips, held, count), lambda i, w: (0, 0, 0))],
            scratch_shapes=[pltpu.VMEM((width, width), jnp.float32)],
        ),
        compiler_params=params(),
        name="prepare",
    )(where, *own, *other)


def project(zt, high, low, overlap):
    vectors, rows = zt.shape
    both = high.shape[0]
    chips, held, more = overlap.shape
    steps = 2

    def kernel(z_ref, high_ref, low_ref, overlap_ref, out_ref):
        sums = dot3(in_two(z_ref[...]), (high_ref[...], low_ref[...]), 1)
        out_ref[:, :, :both] = sums.reshape(chips // steps, held, both)
        out_ref[:, :, both:] = overlap_ref[...]

    return pl.pallas_call(
        kernel,
        out_shape=f32(chips, held, both + more),
        grid=(steps,),
        in_specs=[
            pl.BlockSpec((vectors // steps, rows), lambda i: (i, 0)),
            WHOLE,
            WHOLE,
            pl.BlockSpec((chips // steps, held, more), lambda i: (i, 0, 0)),
        ],
        out_specs=pl.BlockSpec((chips // steps, held, both + more), lambda i: (i, 0, 0)),
        compiler_params=params(),
        name="project",
    )(zt, high, low, overlap)


def add_up(parts):
    def kernel(in_ref, out_ref):
        out_ref[...] = jnp.broadcast_to(jnp.sum(in_ref[...], axis=0, keepdims=True), out_ref.shape)

    return pl.pallas_call(
        kernel,
        out_shape=f32(*parts.shape),
        in_specs=[WHOLE],
        out_specs=WHOLE,
        compiler_params=params(),
        name="add_up",
    )(parts)


def update(where, zt, total, factors, high, low, flip, order, places):
    vectors, rows = zt.shape
    chips, held, _ = total.shape
    block = vectors // (HALVES * places)
    width = high.shape[0] // 2
    cut = width // 2
    count = len(order)
    full = lax.Precision.HIGHEST
    across = (((1,), (1,)), ((), ()))

    def target(w, j):
        return (w[0] ^ flip) * places + partner(w[2], j, w[0], w[1])

    def kernel(where_ref, *refs):
        z_refs, (total_ref, first_ref, second_ref, high_ref, low_ref), outs = (
            refs[:count],
            refs[count:-count],
            refs[-count:],
        )
        sums = [total_ref[times(target(where_ref, j), block // held)] for j in order]
        first, second = (
            jnp.concatenate([v[:, :, at].reshape(block, width) for v in sums], axis=0)
            for at in (slice(0, width), slice(width, 2 * width))
        )
        pieces = total_ref[:, :, 2 * width :].reshape(2, width, cut)
        overlap = jnp.concatenate([pieces[0], pieces[1]], axis=1)
        first = lax.dot_general(first, first_ref[...], across, precision=full)
        second = second - jnp.dot(first, overlap, precision=full)
        second = lax.dot_general(second, second_ref[...], across, precision=full)
        weights = jnp.concatenate([first, second], axis=1)
        change = dot3(in_two(weights), (high_ref[...], low_ref[...]), 0)
        for i in range(count):
            outs[i][...] = z_refs[i][...] - change[i * block : (i + 1) * block]

    def z_spec(j):
        return pl.BlockSpec((block, rows), lambda i, w: (target(w, j), 0))

    return pl.pallas_call(
        kernel,
        out_shape=[f32(block, rows)] * count,
        grid_spec=pltpu.PrefetchScalarGridSpec(
            num_scalar_prefetch=1,
            grid=(1,),
            in_specs=[z_spec(j) for j in order] + [WHOLE] * 5,
            out_specs=[pl.BlockSpec((block, rows), lambda i, w: (0, 0))] * count,
        ),
        compiler_params=params(),
        name="update",
    )(where, *[zt] * count, total, *factors, high, low)


def gather(where, pieces, names, places, out=None):
    block, part = pieces[0].shape
    n = len(pieces)

    def kernel(where_ref, *refs):
        ins, dst, sems = refs[:n], refs[-2], refs[-1]
        copies = []
        for i, (flip, j) in enumerate(names):
            core = where_ref[1] ^ flip
            target = dst.at[times(core, block), times(partner(where_ref[2], j, where_ref[0], core), part)]
            copies.append(pltpu.make_async_copy(ins[i], target, sems.at[i]))
        copy_all(copies)

    held = [] if out is None else [out]
    return pl.pallas_call(
        kernel,
        out_shape=f32(CORES * block, places * part),
        in_specs=[SCALAR] + [ANY] * (n + len(held)),
        out_specs=ANY,
        scratch_shapes=[pltpu.SemaphoreType.DMA((n,))],
        input_output_aliases={n + 1: 0} if held else {},
        compiler_params=params(),
        name="gather",
    )(where, *pieces, *held)


def body(vectors_in, panel_first, panel_second, factor_first, factor_second):
    blocks, places = lax.axis_size("block"), lax.axis_size("place")
    chips = blocks * HALVES * places
    held = vectors_in.shape[0]
    where = jnp.stack([lax.axis_index(name) for name in INNER]).astype(jnp.int32)

    def permute(piece, target):
        index = [(c, h, p) for c in range(CORES) for h in range(HALVES) for p in range(places)]
        return lax.ppermute(piece, INNER, [(i, index.index(target(*at))) for i, at in enumerate(index)])

    order = (3, 1, 0, 2)
    pieces = pack_panels(where, panel_first.T, panel_second.T, order[:2], places)
    pieces += pack_panels(where, panel_first.T, panel_second.T, order[2:], places)
    own = [permute(piece, lambda c, h, p: (h, c, partner(p, j, c, h))) for j, piece in zip(order, pieces)]
    other = [lax.ppermute(piece, "core", [(0, 1), (1, 0)]) for piece in own]
    vectors_in, own, other = lax.optimization_barrier((vectors_in, own, other))
    zt = lax.all_to_all(vectors_in, CHIPS, split_axis=1, concat_axis=0, tiled=True)
    zt = zt.reshape(chips * held, -1)
    zt, own, other = lax.optimization_barrier((zt, own, other))
    high, low, overlap = prepare(where, own, other, order, chips, held)

    partial = project(zt, high, low, overlap)
    parts = lax.all_to_all(partial, CHIPS, split_axis=0, concat_axis=0, tiled=True)
    total = lax.all_to_all(add_up(parts), CHIPS, split_axis=0, concat_axis=0, tiled=True)
    factors = factor_first, factor_second

    pieces, names = [], []
    for flip in range(HALVES):
        for some in (order[:2], order[2:]):
            for j, piece in zip(some, update(where, zt, total, factors, high, low, flip, some, places)):
                pieces.append(permute(piece, lambda c, h, p: (h, c ^ flip, partner(p, j, c, h))))
                names.append((flip, j))
    last = (3, 6, 7)
    out = None
    for some in ([i for i in range(len(pieces)) if i not in last], last):
        out = gather(where, [pieces[i] for i in some], [names[i] for i in some], places, out)
    return out


def solution(mesh):
    rows, cols = mesh.devices.shape
    blocks, places = rows // CORES, cols // HALVES
    split = Mesh(mesh.devices.reshape(blocks, CORES, HALVES, places), ("block",) + INNER)
    row, col = ("block", "core"), ("half", "place")
    return jax.shard_map(
        body,
        mesh=split,
        in_specs=(P(row + col, None), P(row, col), P(row, col), P(), P()),
        out_specs=P(col, row),
        check_vma=False,
    )
```

```python
import jax
import jax.numpy as jnp
from jax import lax
from jax.experimental import pallas as pl
from jax.experimental.pallas import tpu as pltpu
from jax.sharding import Mesh, PartitionSpec as P

CHIPS = ("half", "place", "block")
INNER = ("core", "half", "place")
CORES = 2
HALVES = 2
VMEM_LIMIT = 24 * 1024 * 1024
ANY = pl.BlockSpec(memory_space=pl.ANY)
WHOLE = pl.BlockSpec(memory_space=pltpu.VMEM)
SCALAR = pl.BlockSpec(memory_space=pltpu.SMEM)


def f32(*shape):
    return jax.ShapeDtypeStruct(shape, jnp.float32)


def params():
    return pltpu.CompilerParams(vmem_limit_bytes=VMEM_LIMIT)


def in_two(values):
    high = values.astype(jnp.bfloat16)
    return high, (values - high.astype(jnp.float32)).astype(jnp.bfloat16)


def dot3(left, right, right_dim):
    (lh, ll), (rh, rl) = left, right

    def dot(a, b):
        return lax.dot_general(
            a, b, (((1,), (right_dim,)), ((), ())), preferred_element_type=jnp.float32
        )

    return dot(lh, rh) + (dot(lh, rl) + dot(ll, rh))


def copy_all(copies):
    for one in copies:
        one.start()
    for one in copies:
        one.wait()


def partner(place, j, core, half):
    return place ^ j ^ (2 * (core ^ half))


def times(index, size):
    return pl.ds(pl.multiple_of(index * size, size), size)


def pack_panels(where, first, second, order, places):
    held, rows = first.shape
    part = rows // places
    count = len(order)

    def kernel(where_ref, *refs):
        for i, out in enumerate(refs[2 * count :]):
            out[:held] = refs[2 * i][...]
            out[held:] = refs[2 * i + 1][...]

    def spec(j):
        return pl.BlockSpec((held, part), lambda i, w: (0, partner(w[2], j, w[0], w[1])))

    return pl.pallas_call(
        kernel,
        out_shape=[f32(2 * held, part)] * count,
        grid_spec=pltpu.PrefetchScalarGridSpec(
            num_scalar_prefetch=1,
            grid=(1,),
            in_specs=[spec(j) for j in order for _ in range(2)],
            out_specs=[pl.BlockSpec((2 * held, part), lambda i, w: (0, 0))] * count,
        ),
        compiler_params=params(),
        name="pack_panels",
    )(where, *[first, second] * count)


def prepare(where, own, other, order, chips, held):
    places = len(order)
    held_cols, rows = own[0].shape[0] // 2, own[0].shape[1]
    count = places * held_cols
    width = CORES * count
    steps = 2
    tile = rows // steps

    def kernel(where_ref, *refs):
        ins, (high_ref, low_ref, out_ref, overlap_ref) = refs[: 2 * places], refs[2 * places :]
        step = pl.program_id(0)

        @pl.when(step == 0)
        def _():
            overlap_ref[...] = jnp.zeros_like(overlap_ref)

        for d in range(CORES):
            core = where_ref[0] ^ d
            for i, j in enumerate(order):
                place = partner(where_ref[2], j, core, where_ref[1])
                for p in range(2):
                    at = times((p * CORES + core) * places + place, held_cols)
                    values = ins[d * places + i][pl.ds(p * held_cols, held_cols)]
                    high_ref[at], low_ref[at] = in_two(values)
        first, second = ((high_ref[at], low_ref[at]) for at in (pl.ds(0, width), pl.ds(width, width)))
        overlap_ref[...] += dot3(first, second, 1)

        @pl.when(step == steps - 1)
        def _():
            half = chips // 2
            out_ref[:half] = overlap_ref[:, :count].reshape(half, held, count)
            out_ref[half:] = overlap_ref[:, count:].reshape(half, held, count)

    piece = pl.BlockSpec((2 * held_cols, tile), lambda i, w: (0, i))
    part = pl.BlockSpec((2 * width, tile), lambda i, w: (0, i))
    bf16 = jax.ShapeDtypeStruct((2 * width, rows), jnp.bfloat16)
    return pl.pallas_call(
        kernel,
        out_shape=[bf16, bf16, f32(chips, held, count)],
        grid_spec=pltpu.PrefetchScalarGridSpec(
            num_scalar_prefetch=1,
            grid=(steps,),
            in_specs=[piece] * (2 * places),
            out_specs=[part, part, pl.BlockSpec((chips, held, count), lambda i, w: (0, 0, 0))],
            scratch_shapes=[pltpu.VMEM((width, width), jnp.float32)],
        ),
        compiler_params=params(),
        name="prepare",
    )(where, *own, *other)


def project(zt, high, low, overlap):
    vectors, rows = zt.shape
    both = high.shape[0]
    chips, held, more = overlap.shape
    steps = 2

    def kernel(z_ref, high_ref, low_ref, overlap_ref, out_ref):
        sums = dot3(in_two(z_ref[...]), (high_ref[...], low_ref[...]), 1)
        out_ref[:, :, :both] = sums.reshape(chips // steps, held, both)
        out_ref[:, :, both:] = overlap_ref[...]

    return pl.pallas_call(
        kernel,
        out_shape=f32(chips, held, both + more),
        grid=(steps,),
        in_specs=[
            pl.BlockSpec((vectors // steps, rows), lambda i: (i, 0)),
            WHOLE,
            WHOLE,
            pl.BlockSpec((chips // steps, held, more), lambda i: (i, 0, 0)),
        ],
        out_specs=pl.BlockSpec((chips // steps, held, both + more), lambda i: (i, 0, 0)),
        compiler_params=params(),
        name="project",
    )(zt, high, low, overlap)


def add_up(parts):
    def kernel(in_ref, out_ref):
        out_ref[...] = jnp.broadcast_to(jnp.sum(in_ref[...], axis=0, keepdims=True), out_ref.shape)

    return pl.pallas_call(
        kernel,
        out_shape=f32(*parts.shape),
        in_specs=[WHOLE],
        out_specs=WHOLE,
        compiler_params=params(),
        name="add_up",
    )(parts)


def update(where, zt, total, factors, high, low, flip, order, places):
    vectors, rows = zt.shape
    cols, blocks, held, _ = total.shape
    block = cols * held
    zt = zt.reshape(cols, blocks, held, rows)
    width = high.shape[0] // 2
    cut = width // 2
    count = len(order)
    full = lax.Precision.HIGHEST
    across = (((1,), (1,)), ((), ()))

    def target(w, j):
        return (w[0] ^ flip) * places + partner(w[2], j, w[0], w[1])

    def kernel(where_ref, *refs):
        z_refs, (total_ref, first_ref, second_ref, high_ref, low_ref), outs = (
            refs[:count],
            refs[count:-count],
            refs[-count:],
        )
        sums = [total_ref[:, pl.ds(target(where_ref, j), 1)] for j in order]
        first, second = (
            jnp.concatenate([v[:, :, :, at].reshape(block, width) for v in sums], axis=0)
            for at in (slice(0, width), slice(width, 2 * width))
        )
        pieces = total_ref[:, :, :, 2 * width :].reshape(2, width, cut)
        overlap = jnp.concatenate([pieces[0], pieces[1]], axis=1)
        first = lax.dot_general(first, first_ref[...], across, precision=full)
        second = second - jnp.dot(first, overlap, precision=full)
        second = lax.dot_general(second, second_ref[...], across, precision=full)
        weights = jnp.concatenate([first, second], axis=1)
        change = dot3(in_two(weights), (high_ref[...], low_ref[...]), 0)
        for i in range(count):
            outs[i][...] = z_refs[i][...].reshape(block, rows) - change[i * block : (i + 1) * block]

    def z_spec(j):
        return pl.BlockSpec((cols, 1, held, rows), lambda i, w: (0, target(w, j), 0, 0))

    return pl.pallas_call(
        kernel,
        out_shape=[f32(block, rows)] * count,
        grid_spec=pltpu.PrefetchScalarGridSpec(
            num_scalar_prefetch=1,
            grid=(1,),
            in_specs=[z_spec(j) for j in order] + [WHOLE] * 5,
            out_specs=[pl.BlockSpec((block, rows), lambda i, w: (0, 0))] * count,
        ),
        compiler_params=params(),
        name="update",
    )(where, *[zt] * count, total, *factors, high, low)


def gather(where, pieces, names, places, out=None):
    block, part = pieces[0].shape
    n = len(pieces)

    def kernel(where_ref, *refs):
        ins, dst, sems = refs[:n], refs[-2], refs[-1]
        copies = []
        for i, (flip, j) in enumerate(names):
            core = where_ref[1] ^ flip
            target = dst.at[times(core, block), times(partner(where_ref[2], j, where_ref[0], core), part)]
            copies.append(pltpu.make_async_copy(ins[i], target, sems.at[i]))
        copy_all(copies)

    held = [] if out is None else [out]
    return pl.pallas_call(
        kernel,
        out_shape=f32(CORES * block, places * part),
        in_specs=[SCALAR] + [ANY] * (n + len(held)),
        out_specs=ANY,
        scratch_shapes=[pltpu.SemaphoreType.DMA((n,))],
        input_output_aliases={n + 1: 0} if held else {},
        compiler_params=params(),
        name="gather",
    )(where, *pieces, *held)


def body(vectors_in, panel_first, panel_second, factor_first, factor_second):
    blocks, places = lax.axis_size("block"), lax.axis_size("place")
    chips = blocks * HALVES * places
    held = vectors_in.shape[0]
    where = jnp.stack([lax.axis_index(name) for name in INNER]).astype(jnp.int32)

    def permute(piece, target):
        index = [(c, h, p) for c in range(CORES) for h in range(HALVES) for p in range(places)]
        return lax.ppermute(piece, INNER, [(i, index.index(target(*at))) for i, at in enumerate(index)])

    order = (3, 1, 0, 2)
    pieces = pack_panels(where, panel_first.T, panel_second.T, order[:2], places)
    pieces += pack_panels(where, panel_first.T, panel_second.T, order[2:], places)
    own = [permute(piece, lambda c, h, p: (h, c, partner(p, j, c, h))) for j, piece in zip(order, pieces)]
    other = [lax.ppermute(piece, "core", [(0, 1), (1, 0)]) for piece in own]
    zt = vectors_in.reshape(held, blocks, chips // blocks, -1).transpose(2, 1, 0, 3)
    zt, own, other = lax.optimization_barrier((zt.reshape(chips, held, -1), own, other))
    zt = lax.all_to_all(zt, CHIPS, split_axis=0, concat_axis=0, tiled=True)
    zt = zt.reshape(chips * held, -1)
    zt, own, other = lax.optimization_barrier((zt, own, other))
    high, low, overlap = prepare(where, own, other, order, chips, held)

    partial = project(zt, high, low, overlap)
    parts = lax.all_to_all(partial, CHIPS, split_axis=0, concat_axis=0, tiled=True)
    total = lax.all_to_all(add_up(parts), CHIPS, split_axis=0, concat_axis=0, tiled=True)
    total = total.reshape(chips // blocks, blocks, held, -1)
    factors = factor_first, factor_second

    pieces, names = [], []
    for flip in range(HALVES):
        for some in (order[:2], order[2:]):
            for j, piece in zip(some, update(where, zt, total, factors, high, low, flip, some, places)):
                pieces.append(permute(piece, lambda c, h, p: (h, c ^ flip, partner(p, j, c, h))))
                names.append((flip, j))
    last = (3, 6, 7)
    out = None
    for some in ([i for i in range(len(pieces)) if i not in last], last):
        out = gather(where, [pieces[i] for i in some], [names[i] for i in some], places, out)
    return out


def solution(mesh):
    rows, cols = mesh.devices.shape
    blocks, places = rows // CORES, cols // HALVES
    split = Mesh(mesh.devices.reshape(blocks, CORES, HALVES, places), ("block",) + INNER)
    row, col = ("block", "core"), ("half", "place")
    return jax.shard_map(
        body,
        mesh=split,
        in_specs=(P(row + col, None), P(row, col), P(row, col), P(), P()),
        out_specs=P(col, row),
        check_vma=False,
    )
```

```python
import jax
import jax.numpy as jnp
from jax import lax
from jax.experimental import pallas as pl
from jax.experimental.pallas import tpu as pltpu
from jax.sharding import Mesh, PartitionSpec as P

CHIPS = ("half", "place", "block")
INNER = ("core", "half", "place")
CORES = 2
HALVES = 2
VMEM_LIMIT = 24 * 1024 * 1024
ANY = pl.BlockSpec(memory_space=pl.ANY)
WHOLE = pl.BlockSpec(memory_space=pltpu.VMEM)
SCALAR = pl.BlockSpec(memory_space=pltpu.SMEM)


def f32(*shape):
    return jax.ShapeDtypeStruct(shape, jnp.float32)


def params():
    return pltpu.CompilerParams(vmem_limit_bytes=VMEM_LIMIT)


def in_two(values):
    high = values.astype(jnp.bfloat16)
    return high, (values - high.astype(jnp.float32)).astype(jnp.bfloat16)


def dot3(left, right, right_dim):
    (lh, ll), (rh, rl) = left, right

    def dot(a, b):
        return lax.dot_general(
            a, b, (((1,), (right_dim,)), ((), ())), preferred_element_type=jnp.float32
        )

    return dot(lh, rh) + (dot(lh, rl) + dot(ll, rh))


def copy_all(copies):
    for one in copies:
        one.start()
    for one in copies:
        one.wait()


def partner(place, j, core, half):
    return place ^ j ^ (2 * (core ^ half))


def times(index, size):
    return pl.ds(pl.multiple_of(index * size, size), size)


def pack_panels(where, first, second, order, places):
    held, rows = first.shape
    part = rows // places
    count = len(order)

    def kernel(where_ref, *refs):
        for i, out in enumerate(refs[2 * count :]):
            out[:held] = refs[2 * i][...]
            out[held:] = refs[2 * i + 1][...]

    def spec(j):
        return pl.BlockSpec((held, part), lambda i, w: (0, partner(w[2], j, w[0], w[1])))

    return pl.pallas_call(
        kernel,
        out_shape=[f32(2 * held, part)] * count,
        grid_spec=pltpu.PrefetchScalarGridSpec(
            num_scalar_prefetch=1,
            grid=(1,),
            in_specs=[spec(j) for j in order for _ in range(2)],
            out_specs=[pl.BlockSpec((2 * held, part), lambda i, w: (0, 0))] * count,
        ),
        compiler_params=params(),
        name="pack_panels",
    )(where, *[first, second] * count)


def prepare(where, own, other, order, chips, held):
    places = len(order)
    held_cols, rows = own[0].shape[0] // 2, own[0].shape[1]
    count = places * held_cols
    width = CORES * count
    steps = 2
    tile = rows // steps

    def kernel(where_ref, *refs):
        ins, (high_ref, low_ref, out_ref, overlap_ref) = refs[: 2 * places], refs[2 * places :]
        step = pl.program_id(0)

        @pl.when(step == 0)
        def _():
            overlap_ref[...] = jnp.zeros_like(overlap_ref)

        for d in range(CORES):
            core = where_ref[0] ^ d
            for i, j in enumerate(order):
                place = partner(where_ref[2], j, core, where_ref[1])
                for p in range(2):
                    at = times((p * CORES + core) * places + place, held_cols)
                    values = ins[d * places + i][pl.ds(p * held_cols, held_cols)]
                    high_ref[at], low_ref[at] = in_two(values)
        first, second = ((high_ref[at], low_ref[at]) for at in (pl.ds(0, width), pl.ds(width, width)))
        overlap_ref[...] += dot3(first, second, 1)

        @pl.when(step == steps - 1)
        def _():
            half = chips // 2
            out_ref[:half] = overlap_ref[:, :count].reshape(half, held, count)
            out_ref[half:] = overlap_ref[:, count:].reshape(half, held, count)

    piece = pl.BlockSpec((2 * held_cols, tile), lambda i, w: (0, i))
    part = pl.BlockSpec((2 * width, tile), lambda i, w: (0, i))
    bf16 = jax.ShapeDtypeStruct((2 * width, rows), jnp.bfloat16)
    return pl.pallas_call(
        kernel,
        out_shape=[bf16, bf16, f32(chips, held, count)],
        grid_spec=pltpu.PrefetchScalarGridSpec(
            num_scalar_prefetch=1,
            grid=(steps,),
            in_specs=[piece] * (2 * places),
            out_specs=[part, part, pl.BlockSpec((chips, held, count), lambda i, w: (0, 0, 0))],
            scratch_shapes=[pltpu.VMEM((width, width), jnp.float32)],
        ),
        compiler_params=params(),
        name="prepare",
    )(where, *own, *other)


def project(zt, high, low, overlap):
    vectors, rows = zt.shape
    both = high.shape[0]
    chips, held, more = overlap.shape
    steps = 2

    def kernel(z_ref, high_ref, low_ref, overlap_ref, out_ref):
        sums = dot3(in_two(z_ref[...]), (high_ref[...], low_ref[...]), 1)
        out_ref[:, :, :both] = sums.reshape(chips // steps, held, both)
        out_ref[:, :, both:] = overlap_ref[...]

    return pl.pallas_call(
        kernel,
        out_shape=f32(chips, held, both + more),
        grid=(steps,),
        in_specs=[
            pl.BlockSpec((vectors // steps, rows), lambda i: (i, 0)),
            WHOLE,
            WHOLE,
            pl.BlockSpec((chips // steps, held, more), lambda i: (i, 0, 0)),
        ],
        out_specs=pl.BlockSpec((chips // steps, held, both + more), lambda i: (i, 0, 0)),
        compiler_params=params(),
        name="project",
    )(zt, high, low, overlap)


def add_up(parts):
    def kernel(in_ref, out_ref):
        out_ref[...] = jnp.broadcast_to(jnp.sum(in_ref[...], axis=0, keepdims=True), out_ref.shape)

    return pl.pallas_call(
        kernel,
        out_shape=f32(*parts.shape),
        in_specs=[WHOLE],
        out_specs=WHOLE,
        compiler_params=params(),
        name="add_up",
    )(parts)


def update(where, zt, total, factors, high, low, flip, order, places):
    vectors, rows = zt.shape
    cols, blocks, held, _ = total.shape
    block = cols * held
    zt = zt.reshape(cols, blocks, held, rows)
    width = high.shape[0] // 2
    cut = width // 2
    count = len(order)
    full = lax.Precision.HIGHEST
    across = (((1,), (1,)), ((), ()))

    def target(w, j):
        return (w[0] ^ flip) * places + partner(w[2], j, w[0], w[1])

    def kernel(where_ref, *refs):
        z_refs, (total_ref, first_ref, second_ref, high_ref, low_ref), outs = (
            refs[:count],
            refs[count:-count],
            refs[-count:],
        )
        sums = [total_ref[:, pl.ds(target(where_ref, j), 1)] for j in order]
        first, second = (
            jnp.concatenate([v[:, :, :, at].reshape(block, width) for v in sums], axis=0)
            for at in (slice(0, width), slice(width, 2 * width))
        )
        pieces = total_ref[:, :, :, 2 * width :].reshape(2, width, cut)
        overlap = jnp.concatenate([pieces[0], pieces[1]], axis=1)
        first = lax.dot_general(first, first_ref[...], across, precision=full)
        second = second - jnp.dot(first, overlap, precision=full)
        second = lax.dot_general(second, second_ref[...], across, precision=full)
        weights = jnp.concatenate([first, second], axis=1)
        change = dot3(in_two(weights), (high_ref[...], low_ref[...]), 0)
        for i in range(count):
            outs[i][...] = z_refs[i][...].reshape(block, rows) - change[i * block : (i + 1) * block]

    def z_spec(j):
        return pl.BlockSpec((cols, 1, held, rows), lambda i, w: (0, target(w, j), 0, 0))

    return pl.pallas_call(
        kernel,
        out_shape=[f32(block, rows)] * count,
        grid_spec=pltpu.PrefetchScalarGridSpec(
            num_scalar_prefetch=1,
            grid=(1,),
            in_specs=[z_spec(j) for j in order] + [WHOLE] * 5,
            out_specs=[pl.BlockSpec((block, rows), lambda i, w: (0, 0))] * count,
        ),
        compiler_params=params(),
        name="update",
    )(where, *[zt] * count, total, *factors, high, low)


def gather(where, pieces, names, places, out=None):
    block, part = pieces[0].shape
    n = len(pieces)

    def kernel(where_ref, *refs):
        ins, dst, sems = refs[:n], refs[-2], refs[-1]
        copies = []
        for i, (flip, j) in enumerate(names):
            core = where_ref[1] ^ flip
            target = dst.at[times(core, block), times(partner(where_ref[2], j, where_ref[0], core), part)]
            copies.append(pltpu.make_async_copy(ins[i], target, sems.at[i]))
        copy_all(copies)

    held = [] if out is None else [out]
    return pl.pallas_call(
        kernel,
        out_shape=f32(CORES * block, places * part),
        in_specs=[SCALAR] + [ANY] * (n + len(held)),
        out_specs=ANY,
        scratch_shapes=[pltpu.SemaphoreType.DMA((n,))],
        input_output_aliases={n + 1: 0} if held else {},
        compiler_params=params(),
        name="gather",
    )(where, *pieces, *held)


def body(vectors_in, panel_first, panel_second, factor_first, factor_second):
    blocks, places = lax.axis_size("block"), lax.axis_size("place")
    chips = blocks * HALVES * places
    held = vectors_in.shape[0]
    where = jnp.stack([lax.axis_index(name) for name in INNER]).astype(jnp.int32)

    def permute(piece, target):
        index = [(c, h, p) for c in range(CORES) for h in range(HALVES) for p in range(places)]
        return lax.ppermute(piece, INNER, [(i, index.index(target(*at))) for i, at in enumerate(index)])

    order = (3, 1, 0, 2)
    pieces = pack_panels(where, panel_first.T, panel_second.T, order[:2], places)
    pieces += pack_panels(where, panel_first.T, panel_second.T, order[2:], places)
    own = [permute(piece, lambda c, h, p: (h, c, partner(p, j, c, h))) for j, piece in zip(order, pieces)]
    other = [lax.ppermute(piece, "core", [(0, 1), (1, 0)]) for piece in own]
    zt = vectors_in.reshape(held, blocks, chips // blocks, -1).transpose(2, 1, 0, 3)
    zt, own, other = lax.optimization_barrier((zt.reshape(chips, held, -1), own, other))
    zt = lax.all_to_all(zt, CHIPS, split_axis=0, concat_axis=0, tiled=True)
    zt = zt.reshape(chips * held, -1)
    zt, own, other = lax.optimization_barrier((zt, own, other))
    high, low, overlap = prepare(where, own, other, order, chips, held)

    partial = project(zt, high, low, overlap)
    parts = lax.all_to_all(partial, CHIPS, split_axis=0, concat_axis=0, tiled=True)
    total = lax.all_to_all(add_up(parts), CHIPS, split_axis=0, concat_axis=0, tiled=True)
    total = total.reshape(chips // blocks, blocks, held, -1)
    factors = factor_first, factor_second

    pieces, names = [], []
    for some in (order[:2], order[2:]):
        for flip in range(HALVES):
            for j, piece in zip(some, update(where, zt, total, factors, high, low, flip, some, places)):
                pieces.append(permute(piece, lambda c, h, p: (h, c ^ flip, partner(p, j, c, h))))
                names.append((flip, j))
    last = (5, 6, 7)
    out = None
    for some in ([i for i in range(len(pieces)) if i not in last], last):
        out = gather(where, [pieces[i] for i in some], [names[i] for i in some], places, out)
    return out


def solution(mesh):
    rows, cols = mesh.devices.shape
    blocks, places = rows // CORES, cols // HALVES
    split = Mesh(mesh.devices.reshape(blocks, CORES, HALVES, places), ("block",) + INNER)
    row, col = ("block", "core"), ("half", "place")
    return jax.shard_map(
        body,
        mesh=split,
        in_specs=(P(row + col, None), P(row, col), P(row, col), P(), P()),
        out_specs=P(col, row),
        check_vma=False,
    )
```
